32 devices in a mesh: groups: 2 (over y), chan: 4 (over z), tok: 4 (over x, core).
Axes of the slice: x: 2, y: 2, z: 4, core: 2. Of those that a mesh axis runs over, the one named last changes fastest.
Arguments:
- hidden: bfloat16 [2560, 8192], P(('groups', 'tok'), 'chan'), parts along dimension 0, may hold values from -6 to 6
- norm_gain: bfloat16 [8192], replicated, may hold values from 0.099609375 to 1.8984375
- w_in: bfloat16 [8192, 3, 8192], P('tok', None, 'chan'), may hold values from -0.0625 to 0.0625
- short_taps: float32 [3, 7, 8192], P(None, None, 'chan'), may hold values from -3 to 3
- mr_filter: float32 [512, 128], P('chan'), may hold values from -0.5 to 0.5
- skip_gain: float32 [8192], P('chan'), may hold values from 0.5 to 1.5
- u_store: bfloat16 [64, 127, 8192], P(('groups', 'tok'), None, 'chan'), parts along dimension 0, may hold values from -6 to 6
- z_store: bfloat16 [64, 6, 3, 8192], P(('groups', 'tok'), None, None, 'chan'), parts along dimension 0, may hold values from -6 to 6
- holder: int32 [16], P('groups'), parts along dimension 0, may hold values from 0 to 3
- slot: int32 [16], P('groups'), parts along dimension 0, may hold values from 0 to 7
Outputs:
- gated_out: bfloat16 [2560, 8192], P(('groups', 'tok'), 'chan'), parts along dimension 0
The draws below stay inside these ranges and needn't reach their ends.
There are 2 independent parts, one for each index of `groups`. The reference program is written for one: setup_inputs(seed, part) draws one part's arguments, and reference() takes and returns one part's arrays. A program takes and returns all parts, laid end to end along the dimension named above; an argument that names none is the same for every part. Nothing has to cross between parts.
Inputs may be any that keep to these rules, and one draw needn't show every extreme that they name: `holder`: index of a token shard. Index of a slot on the holder.
All inputs are finite; a program needn't handle non-finite values.
Results may differ from the reference program's by a relative error of at most 0.0086.
Values may be sent and summed in bfloat16 or wider, within the bound.
A program may use at most 448 MiB of HBM per device.

```python
import jax
import jax.numpy as jnp
from jax import lax

D = 8192
GROUP = 16
FILTER = 128
SHORT = 7
NEW = 160
SLOTS = 8
PROMPTS = 8
TOKENS = 1280
GROUPS = 512
ENTRIES = 32
N_TOK = 4


def set_ends(array, own_key, smallest, high):
    longest = array.shape.index(max(array.shape))
    spots = []
    for shift in (0, 1):
        where = [jax.random.randint(jax.random.fold_in(own_key, axis), (), 0, length) for axis, length in enumerate(array.shape)]
        where[longest] = (where[longest] + shift) % array.shape[longest]
        spots.append(tuple(where))
    return array.at[spots[0]].set(smallest).at[spots[1]].set(high)


def shard_levels(rng, extent, shards, smallest, largest):
    loudness, own = 1.0, jax.random.fold_in(rng, 6)
    for position, blocks in shards:
        heights = jnp.exp(jax.random.uniform(jax.random.fold_in(own, position), (blocks,), jnp.float32, smallest / len(shards), largest / len(shards)))
        loudness = loudness * jnp.repeat(heights, extent[position] // blocks).reshape([-1 if axis == position else 1 for axis in range(len(extent))])
    return loudness


def centred(key, extent, deviation, limit, split=(), kind=jnp.bfloat16):
    gain = shard_levels(key, extent, split, -0.22, 0.18) if split else 1.0
    values = jax.random.normal(key, extent, jnp.float32) * deviation * gain
    return jnp.minimum(jnp.maximum(values, -limit), limit).astype(kind)


def setup_inputs(seed: int = 0, part: int = 0) -> dict:
    key_of = jax.random.split(jax.random.key(seed), 11)
    part_keys = jax.random.split(jax.random.fold_in(key_of[10], part), 11)
    hidden = centred(part_keys[0], (TOKENS, D), 1.0, 6.0, ((0, 4), (1, 4)))
    norm_gain = jnp.clip(1.0 + 0.18 * jax.random.normal(key_of[1], (D,), jnp.float32), 0.099609375, 1.8984375).astype(jnp.bfloat16)
    w_in = centred(key_of[2], (D, 3, D), D ** -0.5, 0.0625, ((0, 4), (2, 4)))
    short_taps = centred(key_of[3], (3, SHORT, D), 0.5, 3.0, ((2, 4),), jnp.float32)
    mr_filter = centred(key_of[4], (GROUPS, FILTER), 0.09, 0.5, ((0, 4),), jnp.float32)
    skip_gain = jnp.clip(0.5 + 1.0 * jax.random.uniform(key_of[5], (D,), jnp.float32) ** shard_levels(key_of[5], (D,), ((0, 4),), -0.2, 0.2), 0.5, 1.5)
    u_store = centred(part_keys[6], (ENTRIES, FILTER - 1, D), 1.0, 6.0, ((0, 4), (2, 4)))
    z_store = centred(part_keys[7], (ENTRIES, SHORT - 1, 3, D), 1.0, 6.0, ((0, 4), (3, 4)))
    holder = set_ends(jax.random.randint(part_keys[8], (PROMPTS,), 0, N_TOK), jax.random.fold_in(part_keys[8], 1), 0, N_TOK - 1).astype(jnp.int32)
    slot = set_ends(jax.random.randint(part_keys[9], (PROMPTS,), 0, SLOTS), jax.random.fold_in(part_keys[9], 1), 0, SLOTS - 1).astype(jnp.int32)
    return {"hidden": hidden, "norm_gain": norm_gain, "w_in": w_in, "short_taps": short_taps, "mr_filter": mr_filter, "skip_gain": skip_gain, "u_store": u_store, "z_store": z_store, "holder": holder, "slot": slot}


def short_filter(z_ext, taps):
    count = z_ext.shape[1] - (SHORT - 1)
    total = jnp.zeros((z_ext.shape[0], count, z_ext.shape[2], z_ext.shape[3]), jnp.float32)
    for lag in range(SHORT):
        begin = SHORT - 1 - lag
        total = total + taps[:, lag, :] * z_ext[:, begin:begin + count]
    return total

def long_filter(u_ext, filters):
    prompts, length, chans = u_ext.shape
    count = length - (FILTER - 1)
    rows_t = jnp.arange(count, dtype=jnp.int32)[:, None]
    cols_s = jnp.arange(length, dtype=jnp.int32)[None, :]
    lagged = rows_t + (FILTER - 1) - cols_s
    valid = (lagged >= 0) & (lagged < FILTER)
    table = jnp.take(filters, jnp.clip(lagged, 0, FILTER - 1), axis=1)
    table = jnp.where(valid[None], table, jnp.float32(0.0))
    grouped = u_ext.reshape(prompts, length, chans // GROUP, GROUP)
    result = jnp.einsum('gts,psgc->ptgc', table, grouped, precision=lax.Precision.HIGHEST)
    return result.reshape(prompts, count, chans)

def reference(hidden, norm_gain, w_in, short_taps, mr_filter, skip_gain, u_store, z_store, holder, slot):
    values = hidden.astype(jnp.float32)
    meansq = lax.optimization_barrier(jnp.mean(values * values, axis=-1, keepdims=True))
    normed = (values * lax.rsqrt(meansq + 1e-06) * norm_gain.astype(jnp.float32)).astype(jnp.bfloat16)
    streams = jnp.dot(normed, w_in.reshape(D, 3 * D), preferred_element_type=jnp.float32).astype(jnp.bfloat16)
    streams = streams.reshape(PROMPTS, NEW, 3, D)
    entry = (holder * SLOTS + slot).astype(jnp.int32)
    u_tail = u_store[entry]
    z_tail = z_store[entry]
    z_ext = jnp.concatenate([z_tail, streams], axis=1).astype(jnp.float32)
    filtered = short_filter(z_ext, short_taps)
    gated = (filtered[:, :, 1] * filtered[:, :, 2]).astype(jnp.bfloat16)
    u_ext = jnp.concatenate([u_tail, gated], axis=1).astype(jnp.float32)
    mixed = long_filter(u_ext, mr_filter) + skip_gain * gated.astype(jnp.float32)
    output = (filtered[:, :, 0] * mixed).astype(jnp.bfloat16)
    return output.reshape(TOKENS, D)
```

```python
import functools

import jax
import jax.numpy as jnp
from jax import lax
from jax.experimental import pallas as pl
from jax.experimental.pallas import tpu as pltpu
from jax.sharding import PartitionSpec as P

GROUP = 16
FILTER = 128
SHORT = 7
PAD = 16


def swap(value, count, mask):
    return lax.ppermute(value, "tok", [(i, i ^ mask) for i in range(count)])


def mix_kernel(count, new_len, *refs):
    parts, (z_ref, u_ref, taps_ref, filt_ref, skip_ref, out_ref, z_scr, u_scr) = refs[:count], refs[count:]
    tile = out_ref.shape[1]
    prompts = z_ref.shape[0]
    groups = tile // GROUP
    lane_group = lax.broadcasted_iota(jnp.int32, (FILTER, tile), 1) // GROUP
    rest = new_len - FILTER

    def short(p, s):
        rows = pl.ds(p * new_len, new_len)
        total = parts[0][s, rows, :].astype(jnp.float32)
        for part in parts[1:]:
            total = total + part[s, rows, :].astype(jnp.float32)
        z_scr[0:PAD, :] = z_ref[p, s * PAD : (s + 1) * PAD, :].astype(jnp.float32)
        z_scr[PAD : PAD + new_len, :] = total.astype(jnp.bfloat16).astype(jnp.float32)
        acc = taps_ref[s, 0:1, :] * z_scr[PAD : PAD + new_len, :]
        for lag in range(1, SHORT):
            acc = acc + taps_ref[s, lag : lag + 1, :] * z_scr[PAD - lag : PAD - lag + new_len, :]
        return acc

    for p in range(prompts):
        gated = (short(p, 1) * short(p, 2)).astype(jnp.bfloat16)
        u_scr[0:FILTER, :] = u_ref[p]
        u_scr[FILTER : FILTER + new_len, :] = gated
        early = jnp.zeros((FILTER, tile), jnp.float32)
        late = jnp.zeros((rest, tile), jnp.float32)
        first = u_scr[0 : 2 * FILTER, :]
        second = u_scr[FILTER : FILTER + new_len, :]
        for g in range(groups):
            line = jnp.broadcast_to(filt_ref[g : g + 1, :], (FILTER, 2 * FILTER))
            table = pltpu.roll(line, 0, 1, stride=1, stride_axis=0).astype(jnp.bfloat16)
            a = jnp.dot(table, first, preferred_element_type=jnp.float32)
            b = jnp.dot(table[0:rest, 0:new_len], second, preferred_element_type=jnp.float32)
            early = jnp.where(lane_group == g, a, early)
            late = jnp.where(lane_group[0:rest] == g, b, late)
        mixed = jnp.concatenate([early, late], axis=0) + skip_ref[...] * gated.astype(jnp.float32)
        out_ref[p * new_len : (p + 1) * new_len, :] = (short(p, 0) * mixed).astype(jnp.bfloat16)


def mix(parts, z_tail, u_tail, taps, filters, skip, base, width, new_len):
    rows = parts[0].shape[1]
    prompts = z_tail.shape[0]
    tile = min(256, width)
    off = base // tile
    body = functools.partial(mix_kernel, len(parts), new_len)
    return pl.pallas_call(
        body,
        grid=(width // tile,),
        out_shape=jax.ShapeDtypeStruct((rows, width), jnp.bfloat16),
        in_specs=[pl.BlockSpec((3, rows, tile), lambda i: (0, 0, i)) for _ in parts]
        + [
            pl.BlockSpec((prompts, 3 * PAD, tile), lambda i: (0, 0, i + off)),
            pl.BlockSpec((prompts, FILTER, tile), lambda i: (0, 0, i + off)),
            pl.BlockSpec((3, SHORT, tile), lambda i: (0, 0, i + off)),
            pl.BlockSpec((tile // GROUP, 2 * FILTER), lambda i: (i + off, 0)),
            pl.BlockSpec((1, tile), lambda i: (0, i + off)),
        ],
        out_specs=pl.BlockSpec((rows, tile), lambda i: (0, i)),
        scratch_shapes=[
            pltpu.VMEM((PAD + new_len, tile), jnp.float32),
            pltpu.VMEM((FILTER + new_len, tile), jnp.bfloat16),
        ],
        compiler_params=pltpu.CompilerParams(vmem_limit_bytes=32 * 1024 * 1024),
        cost_estimate=pl.CostEstimate(
            flops=2 * rows * width * 256 * 20, bytes_accessed=rows * width * 32, transcendentals=0
        ),
    )(*parts, z_tail, u_tail, taps, filters, skip)


def tails(u_store, z_store, holder, slot, count, per_shard):
    me = lax.axis_index("tok")
    chans = u_store.shape[2]
    slots = u_store.shape[0]
    z_rows = jnp.transpose(z_store, (0, 2, 1, 3))
    z_rows = jnp.pad(z_rows, ((0, 0), (0, 0), (PAD - (SHORT - 1), 0), (0, 0)))
    z_rows = z_rows.reshape(slots, 3 * PAD, chans)
    u_rows = jnp.pad(u_store, ((0, 0), (1, 0), (0, 0)))
    blocks, keys = [], []
    for s in range(count):
        begin = (me ^ s) * per_shard
        own_slot = lax.dynamic_slice_in_dim(slot, begin, per_shard)
        keys.append(lax.dynamic_slice_in_dim(holder, begin, per_shard))
        rows = [
            jnp.concatenate(
                [
                    lax.dynamic_index_in_dim(u_rows, own_slot[p], 0, keepdims=False),
                    lax.dynamic_index_in_dim(z_rows, own_slot[p], 0, keepdims=False),
                ],
                axis=0,
            )
            for p in range(per_shard)
        ]
        blocks.append(jnp.stack(rows))
    keys = jnp.stack(keys)
    held = jnp.stack(blocks)
    bit = 0
    while (1 << bit) < count:
        mask = 1 << bit
        got = swap(held[1::2], count, mask)
        keys = keys[0::2]
        take = (keys >> bit) == ((me ^ mask) >> bit)
        held = jnp.where(take[:, :, None, None], got, held[0::2])
        bit += 1
    held = held[0]
    return held[:, 0:FILTER], held[:, FILTER:]


def on_device(
    hidden, norm_gain, w_in, short_taps, mr_filter, skip_gain, u_store, z_store, holder, slot
):
    rows = hidden.shape[0]
    chans = hidden.shape[1]
    depth = w_in.shape[0]
    count = lax.axis_size("tok")
    me = lax.axis_index("tok")
    per_shard = holder.shape[0] // count
    new_len = rows // per_shard
    u_tail, z_tail = tails(u_store, z_store, holder, slot, count, per_shard)
    weights = jnp.transpose(w_in, (1, 0, 2))
    filters = jnp.pad(mr_filter[:, ::-1], ((0, 0), (1, FILTER - 1)))
    skip = skip_gain.reshape(1, chans)
    gain = norm_gain.astype(jnp.float32)
    chunks = max(1, min(4, chans // 512))
    width = chans // chunks
    order = [s for s in range(count) if s & 1] + [s for s in range(count) if not s & 1]
    half = count // 2
    wholes = [
        lax.all_gather(hidden[p * new_len : (p + 1) * new_len], "chan", axis=1, tiled=True)
        for p in range(per_shard)
    ]
    results = []
    for p in range(per_shard):
        values = wholes[p].astype(jnp.float32)
        meansq = jnp.mean(values * values, axis=-1, keepdims=True)
        normed = (values * lax.rsqrt(meansq + 1e-06) * gain).astype(jnp.bfloat16)
        got = {}
        for s in range(count):
            mine = lax.dynamic_slice_in_dim(normed, (me ^ s) * depth, depth, 1)
            got[s] = mine if s == 0 else swap(mine, count, s)
        leave = jnp.concatenate([got[s] for s in order[:half]], axis=0)
        keep = jnp.concatenate([got[s] for s in order[half:]], axis=0)
        pieces = []
        for c in range(chunks):
            part = weights[:, :, c * width : (c + 1) * width]
            sent = jnp.stack(
                [jnp.dot(leave, part[s], preferred_element_type=jnp.float32) for s in range(3)]
            ).astype(jnp.bfloat16)
            kept = jnp.stack(
                [jnp.dot(keep, part[s], preferred_element_type=jnp.float32) for s in range(3)]
            )
            held = kept.reshape(3, half, new_len, width)
            back = swap(sent, count, 1).reshape(3, half, new_len, width)
            bit = 1
            while (1 << bit) < count:
                now = held + back.astype(jnp.float32)
                out = now[:, 1::2].astype(jnp.bfloat16)
                held = now[:, 0::2]
                back = swap(out, count, 1 << bit)
                bit += 1
            pieces.append(
                mix(
                    [held[:, 0], back[:, 0]],
                    z_tail[p : p + 1],
                    u_tail[p : p + 1],
                    short_taps,
                    filters,
                    skip,
                    c * width,
                    width,
                    new_len,
                )
            )
        results.append(jnp.concatenate(pieces, axis=1))
    return jnp.concatenate(results, axis=0)


def solution(mesh):
    placed = (
        P(("groups", "tok"), "chan"),
        P(),
        P("tok", None, "chan"),
        P(None, None, "chan"),
        P("chan", None),
        P("chan"),
        P(("groups", "tok"), None, "chan"),
        P(("groups", "tok"), None, None, "chan"),
        P("groups"),
        P("groups"),
    )
    return jax.shard_map(
        on_device,
        mesh=mesh,
        in_specs=placed,
        out_specs=P(("groups", "tok"), "chan"),
        check_vma=False,
    )
```

```python
import functools

import jax
import jax.numpy as jnp
from jax import lax
from jax.experimental import pallas as pl
from jax.experimental.pallas import tpu as pltpu
from jax.sharding import PartitionSpec as P

GROUP = 16
FILTER = 128
SHORT = 7
PAD = 16


def swap(value, count, mask):
    return lax.ppermute(value, "tok", [(i, i ^ mask) for i in range(count)])


def mix_kernel(count, new_len, *refs):
    parts, (z_ref, u_ref, taps_ref, filt_ref, skip_ref, out_ref, z_scr, u_scr) = refs[:count], refs[count:]
    tile = out_ref.shape[1]
    prompts = z_ref.shape[0]
    groups = tile // GROUP
    lane_group = lax.broadcasted_iota(jnp.int32, (FILTER, tile), 1) // GROUP
    rest = new_len - FILTER

    def short(p, s):
        rows = pl.ds(p * new_len, new_len)
        total = parts[0][s, 0, rows, :].astype(jnp.float32)
        for part in parts[1:]:
            total = total + part[s, 0, rows, :].astype(jnp.float32)
        z_scr[0:PAD, :] = z_ref[p, s * PAD : (s + 1) * PAD, :].astype(jnp.float32)
        z_scr[PAD : PAD + new_len, :] = total.astype(jnp.bfloat16).astype(jnp.float32)
        acc = taps_ref[s, 0:1, :] * z_scr[PAD : PAD + new_len, :]
        for lag in range(1, SHORT):
            acc = acc + taps_ref[s, lag : lag + 1, :] * z_scr[PAD - lag : PAD - lag + new_len, :]
        return acc

    for p in range(prompts):
        gated = (short(p, 1) * short(p, 2)).astype(jnp.bfloat16)
        u_scr[0:FILTER, :] = u_ref[p]
        u_scr[FILTER : FILTER + new_len, :] = gated
        early = jnp.zeros((FILTER, tile), jnp.float32)
        late = jnp.zeros((rest, tile), jnp.float32)
        first = u_scr[0 : 2 * FILTER, :]
        second = u_scr[FILTER : FILTER + new_len, :]
        for g in range(groups):
            line = jnp.broadcast_to(filt_ref[g : g + 1, :], (FILTER, 2 * FILTER))
            table = pltpu.roll(line, 0, 1, stride=1, stride_axis=0).astype(jnp.bfloat16)
            a = jnp.dot(table, first, preferred_element_type=jnp.float32)
            b = jnp.dot(table[0:rest, 0:new_len], second, preferred_element_type=jnp.float32)
            early = jnp.where(lane_group == g, a, early)
            late = jnp.where(lane_group[0:rest] == g, b, late)
        mixed = jnp.concatenate([early, late], axis=0) + skip_ref[...] * gated.astype(jnp.float32)
        out_ref[p * new_len : (p + 1) * new_len, :] = (short(p, 0) * mixed).astype(jnp.bfloat16)


def project_kernel(x_ref, w_ref, sent_ref, kept_ref):
    half = sent_ref.shape[1]
    sent_ref[0] = jnp.dot(
        x_ref[0:half, :], w_ref[0], preferred_element_type=jnp.float32
    ).astype(jnp.bfloat16)
    kept_ref[0] = jnp.dot(x_ref[half:, :], w_ref[0], preferred_element_type=jnp.float32)


def project(x, weights, base, width):
    rows, depth = x.shape
    half = rows // 2
    off = base // width
    return pl.pallas_call(
        project_kernel,
        grid=(3,),
        out_shape=(
            jax.ShapeDtypeStruct((3, half, width), jnp.bfloat16),
            jax.ShapeDtypeStruct((3, half, width), jnp.float32),
        ),
        in_specs=[
            pl.BlockSpec((rows, depth), lambda i: (0, 0)),
            pl.BlockSpec((1, depth, width), lambda i: (i, 0, off)),
        ],
        out_specs=(
            pl.BlockSpec((1, half, width), lambda i: (i, 0, 0)),
            pl.BlockSpec((1, half, width), lambda i: (i, 0, 0)),
        ),
        compiler_params=pltpu.CompilerParams(vmem_limit_bytes=40 * 1024 * 1024),
        cost_estimate=pl.CostEstimate(
            flops=6 * rows * depth * width,
            bytes_accessed=6 * depth * width + 2 * rows * depth + 9 * rows * width,
            transcendentals=0,
        ),
    )(x, weights)


def mix(parts, z_tail, u_tail, taps, filters, skip, base, width, new_len):
    rows = parts[0].shape[2]
    prompts = z_tail.shape[0]
    tile = min(256, width)
    off = base // tile
    body = functools.partial(mix_kernel, len(parts), new_len)
    return pl.pallas_call(
        body,
        grid=(width // tile,),
        out_shape=jax.ShapeDtypeStruct((rows, width), jnp.bfloat16),
        in_specs=[pl.BlockSpec((3, 1, rows, tile), lambda i: (0, 0, 0, i)) for _ in parts]
        + [
            pl.BlockSpec((prompts, 3 * PAD, tile), lambda i: (0, 0, i + off)),
            pl.BlockSpec((prompts, FILTER, tile), lambda i: (0, 0, i + off)),
            pl.BlockSpec((3, SHORT, tile), lambda i: (0, 0, i + off)),
            pl.BlockSpec((tile // GROUP, 2 * FILTER), lambda i: (i + off, 0)),
            pl.BlockSpec((1, tile), lambda i: (0, i + off)),
        ],
        out_specs=pl.BlockSpec((rows, tile), lambda i: (0, i)),
        scratch_shapes=[
            pltpu.VMEM((PAD + new_len, tile), jnp.float32),
            pltpu.VMEM((FILTER + new_len, tile), jnp.bfloat16),
        ],
        compiler_params=pltpu.CompilerParams(vmem_limit_bytes=32 * 1024 * 1024),
        cost_estimate=pl.CostEstimate(
            flops=2 * rows * width * 256 * 20, bytes_accessed=rows * width * 32, transcendentals=0
        ),
    )(*parts, z_tail, u_tail, taps, filters, skip)


def tails(u_store, z_store, holder, slot, count, per_shard):
    me = lax.axis_index("tok")
    chans = u_store.shape[2]
    slots = u_store.shape[0]
    z_rows = jnp.transpose(z_store, (0, 2, 1, 3))
    z_rows = jnp.pad(z_rows, ((0, 0), (0, 0), (PAD - (SHORT - 1), 0), (0, 0)))
    z_rows = z_rows.reshape(slots, 3 * PAD, chans)
    u_rows = jnp.pad(u_store, ((0, 0), (1, 0), (0, 0)))
    blocks, keys = [], []
    for s in range(count):
        begin = (me ^ s) * per_shard
        own_slot = lax.dynamic_slice_in_dim(slot, begin, per_shard)
        keys.append(lax.dynamic_slice_in_dim(holder, begin, per_shard))
        rows = [
            jnp.concatenate(
                [
                    lax.dynamic_index_in_dim(u_rows, own_slot[p], 0, keepdims=False),
                    lax.dynamic_index_in_dim(z_rows, own_slot[p], 0, keepdims=False),
                ],
                axis=0,
            )
            for p in range(per_shard)
        ]
        blocks.append(jnp.stack(rows))
    keys = jnp.stack(keys)
    held = jnp.stack(blocks)
    bit = 0
    begun = held
    while (1 << bit) < count:
        mask = 1 << bit
        begun = held
        got = swap(held[1::2], count, mask)
        keys = keys[0::2]
        take = (keys >> bit) == ((me ^ mask) >> bit)
        held = jnp.where(take[:, :, None, None], got, held[0::2])
        bit += 1
    held = held[0]
    return held[:, 0:FILTER], held[:, FILTER:], begun


def on_device(
    hidden, norm_gain, w_in, short_taps, mr_filter, skip_gain, u_store, z_store, holder, slot
):
    rows = hidden.shape[0]
    chans = hidden.shape[1]
    depth = w_in.shape[0]
    count = lax.axis_size("tok")
    me = lax.axis_index("tok")
    per_shard = holder.shape[0] // count
    new_len = rows // per_shard
    u_tail, z_tail, begun = tails(u_store, z_store, holder, slot, count, per_shard)
    weights = jnp.transpose(w_in, (1, 0, 2))
    filters = jnp.pad(mr_filter[:, ::-1], ((0, 0), (1, FILTER - 1)))
    skip = skip_gain.reshape(1, chans)
    gain = norm_gain.astype(jnp.float32)
    chunks = max(1, min(4, chans // 512))
    width = chans // chunks
    order = [s for s in range(count) if s & 1] + [s for s in range(count) if not s & 1]
    half = count // 2
    wholes = [
        lax.all_gather(hidden[p * new_len : (p + 1) * new_len], "chan", axis=1, tiled=True)
        for p in range(per_shard)
    ]
    results = []
    after = begun
    landed = []
    for p in range(per_shard):
        whole = wholes[p]
        whole, _ = lax.optimization_barrier((whole, after))
        values = whole.astype(jnp.float32)
        meansq = jnp.mean(values * values, axis=-1, keepdims=True)
        normed = (values * lax.rsqrt(meansq + 1e-06) * gain).astype(jnp.bfloat16)
        got = {}
        for s in range(count):
            mine = lax.dynamic_slice_in_dim(normed, (me ^ s) * depth, depth, 1)
            got[s] = mine if s == 0 else swap(mine, count, s)
        rows_in = jnp.concatenate([got[s] for s in order], axis=0)
        if results:
            rows_in, _ = lax.optimization_barrier((rows_in, results[-1][:-1]))
        pieces = []
        for c in range(chunks):
            if len(landed) >= 3:
                rows_in, _ = lax.optimization_barrier((rows_in, landed[-3]))
            sent, kept = project(rows_in, weights, c * width, width)
            after = kept
            kept = kept.reshape(3, half, new_len, width)
            back = swap(sent, count, 1).reshape(3, half, new_len, width)
            parts, now = [kept, back], [kept, back]
            bit = 1
            while (1 << bit) < count:
                out = sum(part[:, 1::2].astype(jnp.float32) for part in now).astype(jnp.bfloat16)
                back = swap(out, count, 1 << bit)
                now = [part[:, 0::2] for part in now] + [back]
                parts.append(back)
                bit += 1
            landed.append(back)
            pieces.append(
                mix(
                    parts,
                    z_tail[p : p + 1],
                    u_tail[p : p + 1],
                    short_taps,
                    filters,
                    skip,
                    c * width,
                    width,
                    new_len,
                )
            )
        results.append(pieces)
    return jnp.concatenate([jnp.concatenate(line, axis=1) for line in results], axis=0)


def solution(mesh):
    placed = (
        P(("groups", "tok"), "chan"),
        P(),
        P("tok", None, "chan"),
        P(None, None, "chan"),
        P("chan", None),
        P("chan"),
        P(("groups", "tok"), None, "chan"),
        P(("groups", "tok"), None, None, "chan"),
        P("groups"),
        P("groups"),
    )
    return jax.shard_map(
        on_device,
        mesh=mesh,
        in_specs=placed,
        out_specs=P(("groups", "tok"), "chan"),
        check_vma=False,
    )
```
